32 devices in a mesh: pipe: 2 (over core), seq: 4 (over y, x), tensor: 4 (over z).
Axes of the slice: x: 2, y: 2, z: 4, core: 2. Of those that a mesh axis runs over, the one named last changes fastest.
Arguments:
- token_ids: int32 [2, 768], P(None, 'seq'), may hold values from 0 to 511
- embed_table: bfloat16 [512, 8192], P(None, 'tensor'), may hold values from -24 to 24
- in_proj: bfloat16 [2, 8192, 3, 4096], P('pipe', None, None, 'tensor'), may hold values from -0.0625 to 0.0625
- feat_taps: float32 [2, 3, 3, 4096], P('pipe', None, None, 'tensor'), may hold values from -3 to 3
- se_taps: float32 [7, 4096], P(None, 'tensor'), may hold values from -2 to 2
- mr_taps: float32 [128, 4096], P(None, 'tensor'), may hold values from -0.6 to 0.6
- out_proj: bfloat16 [2, 4096, 8192], P('pipe', 'tensor'), may hold values from -0.125 to 0.125
- norm_gain: bfloat16 [2, 8192], P('pipe', 'tensor'), may hold values from 0.25 to 1.75
Outputs:
- segment_out: bfloat16 [2, 2, 768, 8192], P('pipe', None, 'seq', 'tensor')
The draws below stay inside these ranges and needn't reach their ends.
All inputs are finite; a program needn't handle non-finite values.
Results may differ from the reference program's by a relative error of at most 0.023.
Values may be sent and summed in bfloat16 or wider, within the bound.
A program may use at most 192 MiB of HBM per device.

```python
import math
import jax
import jax.numpy as jnp
from jax import lax

D = 8192
VOCAB = 512
CH = 4096
KL = 128
KS = 7
KF = 3
SEGMENTS = 2
SLICES = 2
SEQLEN = 768
N_TENSOR = 4


def draw_embed_table(key, part):
    key_base, key_rows, key_cols = jax.random.split(key, 3)
    col_scale = jnp.exp(jax.random.uniform(key_cols, (1, D), jnp.float32, math.log(0.5), math.log(2.0)))
    normal_part = jnp.clip(jax.random.normal(key_base, (VOCAB, D), jnp.float32), -4.0, 4.0)
    row_scale = jnp.exp(jax.random.uniform(key_rows, (VOCAB, 1), jnp.float32, math.log(0.3), math.log(3.0)))
    return (normal_part * row_scale * col_scale).astype(jnp.bfloat16)


def draw_mr_taps(key, part):
    key_taps, key_rate = jax.random.split(key, 2)
    decay_rate = jnp.exp(jax.random.uniform(key_rate, (1, CH), jnp.float32, math.log(1.0 / 600.0), math.log(1.0 / 25.0)))
    normal_part = jnp.clip(jax.random.normal(key_taps, (KL, CH), jnp.float32), -4.0, 4.0)
    positions = jnp.arange(KL, dtype=jnp.float32)[:, None]
    return (0.15 * normal_part * jnp.exp(-decay_rate * positions)).astype(jnp.float32)


def place_ends(result, stream_key, least, top_value):
    longest = result.shape.index(max(result.shape))
    spots = []
    for shift in (0, 1):
        where = [jax.random.randint(jax.random.fold_in(stream_key, axis), (), 0, length) for axis, length in enumerate(result.shape)]
        where[longest] = (where[longest] + shift) % result.shape[longest]
        spots.append(tuple(where))
    return result.at[spots[0]].set(least).at[spots[1]].set(top_value)


def strengthened(array, stream_key, source, target, shards_of, factor):
    owner, partner = [(jnp.arange(array.shape[dim]) // (array.shape[dim] // shards_of)).reshape([-1 if axis == dim else 1 for axis in range(array.ndim)]) for dim in (source, target)]
    chosen = jax.random.permutation(stream_key, shards_of)[partner]
    strong = (owner == chosen) | (owner == (partner + shards_of // 2) % shards_of)
    return jnp.where(strong, factor * array, array)


def level_of(rng, shape, cuts, smallest, high):
    def one(dim, blocks):
        heights = jax.random.uniform(jax.random.fold_in(jax.random.fold_in(rng, 6), dim), (blocks,), jnp.float32, smallest / len(cuts), high / len(cuts))
        return jnp.repeat(jnp.exp(heights), shape[dim] // blocks).reshape((-1,) + (1,) * (len(shape) - dim - 1))

    factor_of = one(*cuts[0])
    for cut in cuts[1:]:
        factor_of = factor_of * one(*cut)
    return factor_of


def gaussian(own_key, extent, scale, bound, shards=(), kind=jnp.bfloat16):
    factor_of = level_of(own_key, extent, shards, -0.22, 0.18) if shards else 1.0
    array = jax.random.normal(own_key, extent, jnp.float32) * scale * factor_of
    return jnp.minimum(jnp.maximum(array, -bound), bound).astype(kind)


def gaussian_with(own_key, extent, deviation, bound, cuts, heavy, held_as=jnp.bfloat16):
    drawn = deviation * jax.random.normal(own_key, extent, jnp.float32)
    if cuts:
        drawn = drawn * level_of(own_key, extent, cuts, -0.22, 0.18)
    return jnp.clip(strengthened(drawn, jax.random.fold_in(own_key, 3), *heavy), -bound, bound).astype(held_as)


def setup_inputs(seed: int = 0) -> dict:
    seeds = jax.random.split(jax.random.key(seed), 9)
    token_ids = place_ends(jax.random.randint(seeds[0], (SLICES, SEQLEN), 0, VOCAB), jax.random.fold_in(seeds[0], 1), 0, VOCAB - 1).astype(jnp.int32)
    embed_table = draw_embed_table(jax.random.fold_in(seeds[8], 71), 0)
    in_proj = gaussian(seeds[2], (SEGMENTS, D, 3, CH), D ** -0.5, 0.0625, ((0, 2), (3, 4)))
    feat_taps = gaussian(seeds[3], (SEGMENTS, KF, 3, CH), 0.6, 3.0, ((0, 2), (3, 4)), jnp.float32)
    se_taps = gaussian(seeds[4], (KS, CH), 0.4, 2.0, ((1, 4),), jnp.float32)
    mr_taps = draw_mr_taps(jax.random.fold_in(seeds[8], 71), 0)
    out_proj = gaussian_with(seeds[6], (SEGMENTS, CH, D), CH ** -0.5, 0.125, ((0, 2), (1, 4)), (1, 2, 4, 2.0))
    norm_gain = jnp.clip(1.0 + 0.15 * jax.random.normal(seeds[7], (SEGMENTS, D), jnp.float32), 0.25, 1.75).astype(jnp.bfloat16)
    return dict(token_ids=token_ids, embed_table=embed_table, in_proj=in_proj, feat_taps=feat_taps, se_taps=se_taps, mr_taps=mr_taps, out_proj=out_proj, norm_gain=norm_gain)


epsilon = 1e-06

def hyena_layer(stream_in, in_weights, feat_weights, long_taps, out_weights, gain_row):
    window = stream_in.shape[0]
    values = stream_in.astype(jnp.float32)
    inv_rms = lax.rsqrt(lax.optimization_barrier(jnp.mean(values * values, axis=1, keepdims=True)) + epsilon)
    normed = (values * inv_rms * gain_row.astype(jnp.float32)[None, :]).astype(jnp.bfloat16)
    projected = jnp.dot(normed, in_weights.reshape(D, 3 * CH), preferred_element_type=jnp.float32).astype(jnp.bfloat16)
    raw_padded = jnp.pad(projected.astype(jnp.float32), ((KF - 1, 0), (0, 0)))
    feat_flat = feat_weights.reshape(KF, 3 * CH).astype(jnp.float32)
    featured = jnp.zeros((window, 3 * CH), jnp.float32)
    for tap_index in range(KF):
        featured = featured + feat_flat[tap_index][None, :] * raw_padded[KF - 1 - tap_index:KF - 1 - tap_index + window]
    q_feat = featured[:, :CH]
    gated_kv = featured[:, CH:2 * CH] * featured[:, 2 * CH:]
    gated_pad = jnp.pad(gated_kv, ((KL - 1, 0), (0, 0)))

    def add_tap(tap_index, running):
        shifted = lax.dynamic_slice_in_dim(gated_pad, KL - 1 - tap_index, window, 0)
        return running + long_taps[tap_index][None, :] * shifted
    filtered = lax.fori_loop(0, KL, add_tap, jnp.zeros((window, CH), jnp.float32))
    y_out = (q_feat * filtered).astype(jnp.bfloat16)
    group = CH // N_TENSOR
    y_groups = jnp.transpose(y_out.reshape(window, N_TENSOR, group), (1, 0, 2))
    w_groups = out_weights.reshape(N_TENSOR, group, D)

    def add_group(running, pair):
        part = jnp.dot(pair[0], pair[1], preferred_element_type=jnp.float32).astype(jnp.bfloat16)
        part = lax.optimization_barrier(part)
        return (running + part.astype(jnp.float32), None)
    mixed, _ = lax.scan(add_group, jnp.zeros((window, D), jnp.float32), (y_groups, w_groups))
    return (values + mixed).astype(jnp.bfloat16)

def reference(token_ids, embed_table, in_proj, feat_taps, se_taps, mr_taps, out_proj, norm_gain):
    flat_ids = token_ids.reshape(-1).astype(jnp.int32)
    embedded = jnp.take(embed_table, flat_ids, axis=0)
    se_full = jnp.concatenate([se_taps.astype(jnp.float32), jnp.zeros((KL - KS, CH), jnp.float32)], axis=0)
    first_out = hyena_layer(embedded, in_proj[0], feat_taps[0], se_full, out_proj[0], norm_gain[0])
    second_out = hyena_layer(first_out, in_proj[1], feat_taps[1], mr_taps.astype(jnp.float32), out_proj[1], norm_gain[1])
    stacked = jnp.stack([first_out, second_out], axis=0)
    return stacked.reshape(SEGMENTS, SLICES, SEQLEN, D)
```

```python
import functools

import jax
import jax.numpy as jnp
from jax import lax
from jax.experimental import pallas as pl
from jax.experimental.pallas import tpu as pltpu
from jax.sharding import PartitionSpec as P

KL = 128
KS = 7
KF = 3
HEAD = 16
TAPS_AT_ONCE = 4
VMEM_LIMIT = 50 * 1024 * 1024


epsilon = 1e-06


def pairs_on(section, axis, links):
    count = lax.axis_size(axis)
    base = section * count
    return [(base + source, base + target) for source, target in links]


def send_on(value, section, axis, links):
    return lax.ppermute(value, ("pipe", axis), pairs_on(section, axis, links))


def gather_features(block, section):
    count = lax.axis_size("tensor")
    if count > 4:
        return lax.all_gather(block, "tensor", axis=0)
    place = lax.axis_index("tensor")
    up, down = [block], [block]
    for step in range(1, count):
        up.append(send_on(up[-1], section, "tensor", [(i, i + 1) for i in range(step - 1, count - 1)]))
        down.append(send_on(down[-1], section, "tensor", [(i, i - 1) for i in range(1, count - step + 1)]))
    whole = []
    for owner in range(count):
        value = block
        for step in range(1, count - owner):
            value = jnp.where(place == owner + step, up[step], value)
        for step in range(1, owner + 1):
            value = jnp.where(place == owner - step, down[step], value)
        whole.append(value)
    return jnp.stack(whole, axis=0)


def scatter_sum(partial, section):
    count = lax.axis_size("tensor")
    place = lax.axis_index("tensor")
    if count > 4:
        own = lax.psum_scatter(partial, "tensor", scatter_dimension=2, tiled=False)
        return own.astype(jnp.float32)

    def block(index):
        index = jnp.clip(index, 0, count - 1)
        return lax.dynamic_index_in_dim(partial, index, 2, keepdims=False).astype(jnp.float32)

    up = down = None
    for step in range(1, count):
        up_block = block(count - step + place)
        down_block = block(step - count + place)
        if step > 1:
            up_block = up_block + up.astype(jnp.float32)
            down_block = down_block + down.astype(jnp.float32)
        up = send_on(up_block.astype(jnp.bfloat16), section, "tensor", [(i, i + 1) for i in range(step)])
        down = send_on(
            down_block.astype(jnp.bfloat16), section, "tensor", [(i, i - 1) for i in range(count - step, count)]
        )
    total = block(place)
    if up is not None:
        total = total + up.astype(jnp.float32) + down.astype(jnp.float32)
    return total


def project_kernel(x_ref, w_ref, inv_ref, out_ref, total):
    step = pl.program_id(1)

    @pl.when(step == 0)
    def _():
        total[...] = jnp.zeros_like(total)

    total[...] += jnp.dot(x_ref[0], w_ref[0], preferred_element_type=jnp.float32)

    @pl.when(step == pl.num_programs(1) - 1)
    def _():
        out_ref[...] = (total[...] * inv_ref[...]).astype(out_ref.dtype)


def project(gathered, weights, inv_rms):
    count, rows, width = gathered.shape
    groups, depth, channels = weights.shape
    tile = min(width, 1024)
    per_block = width // tile
    return pl.pallas_call(
        project_kernel,
        grid=(groups, depth // tile),
        in_specs=[
            pl.BlockSpec((1, rows, tile), lambda g, k: (k // per_block, 0, k % per_block)),
            pl.BlockSpec((1, tile, channels), lambda g, k: (g, k, 0)),
            pl.BlockSpec((rows, 1), lambda g, k: (0, 0)),
        ],
        out_specs=pl.BlockSpec((rows, channels), lambda g, k: (0, g)),
        out_shape=jax.ShapeDtypeStruct((rows, groups * channels), jnp.bfloat16),
        scratch_shapes=[pltpu.VMEM((rows, channels), jnp.float32)],
        compiler_params=pltpu.CompilerParams(vmem_limit_bytes=VMEM_LIMIT),
        cost_estimate=pl.CostEstimate(
            flops=2 * rows * depth * groups * channels,
            bytes_accessed=2 * (groups * depth * channels + rows * depth),
            transcendentals=0,
        ),
    )(gathered, weights, inv_rms)


def mix_kernel(taps_count, has_history, *refs):
    if has_history:
        q_ref, k_ref, v_ref, history_ref, feat_ref, taps_ref, out_ref, wide, gated, shifted = refs
    else:
        q_ref, k_ref, v_ref, feat_ref, taps_ref, out_ref, wide, gated, shifted = refs
    rows = out_ref.shape[1]
    span = KL + rows

    def featured(ref, which, back):
        wide[...] = ref[0].astype(jnp.float32)
        value = jnp.zeros((back + rows, wide.shape[1]), jnp.float32)
        for tap in range(KF):
            value = value + feat_ref[tap, which : which + 1, :] * wide[
                HEAD - back - tap : HEAD - tap + rows, :
            ]
        return value

    back = 0 if has_history else 8
    gated[KL - back :, :] = featured(k_ref, 1, back) * featured(v_ref, 2, back)
    if has_history:
        gated[:KL, :] = history_ref[0].astype(jnp.float32)
    phases = min(8, taps_count)
    for phase in range(phases):
        start = 8 if has_history else KL
        shifted[phase, start:, :] = gated[start - phase : span - phase, :]

    lanes = out_ref.shape[2]
    if taps_count <= 8:
        total = jnp.zeros((rows, lanes), jnp.float32)
        for phase in range(phases):
            total = total + taps_ref[phase : phase + 1, :] * shifted[phase, KL:, :]
    else:

        def body(step, total):
            base = pl.multiple_of(step * (8 * TAPS_AT_ONCE), 8 * TAPS_AT_ONCE)
            taps = taps_ref[pl.ds(base, 8 * TAPS_AT_ONCE), :]
            start = pl.multiple_of(KL - 8 * (TAPS_AT_ONCE - 1) - base, 8)
            for phase in range(8):
                window = shifted[phase, pl.ds(start, rows + 8 * (TAPS_AT_ONCE - 1)), :]
                for late in range(TAPS_AT_ONCE):
                    offset = 8 * (TAPS_AT_ONCE - 1 - late)
                    tap = 8 * late + phase
                    total = total + taps[tap : tap + 1, :] * window[offset : offset + rows, :]
            return total

        total = lax.fori_loop(
            0, taps_count // (8 * TAPS_AT_ONCE), body, jnp.zeros((rows, lanes), jnp.float32)
        )
    out_ref[0] = (featured(q_ref, 0, 0) * total).astype(out_ref.dtype)


def mix(extended, history, feat_taps, taps):
    slices, length, wide_channels = extended.shape
    channels = wide_channels // 3
    rows = length - HEAD
    lanes = 128
    blocks = channels // lanes
    in_specs = [
        pl.BlockSpec((1, length, lanes), functools.partial(lambda g, s, c: (s, 0, g * blocks + c), g))
        for g in range(3)
    ]
    operands = [extended, extended, extended]
    if history is not None:
        in_specs.append(pl.BlockSpec((1, KL, lanes), lambda s, c: (s, 0, c)))
        operands.append(history)
    in_specs.append(pl.BlockSpec((KF, 3, lanes), lambda s, c: (0, 0, c)))
    in_specs.append(pl.BlockSpec((taps.shape[0], lanes), lambda s, c: (0, c)))
    operands += [feat_taps, taps]
    return pl.pallas_call(
        functools.partial(mix_kernel, taps.shape[0], history is not None),
        grid=(slices, blocks),
        in_specs=in_specs,
        out_specs=pl.BlockSpec((1, rows, lanes), lambda s, c: (s, 0, c)),
        out_shape=jax.ShapeDtypeStruct((slices, rows, channels), jnp.bfloat16),
        scratch_shapes=[
            pltpu.VMEM((length, lanes), jnp.float32),
            pltpu.VMEM((KL + rows, lanes), jnp.float32),
            pltpu.VMEM((8, KL + rows, lanes), jnp.float32),
        ],
        compiler_params=pltpu.CompilerParams(vmem_limit_bytes=VMEM_LIMIT),
        cost_estimate=pl.CostEstimate(
            flops=2 * taps.shape[0] * slices * rows * channels,
            bytes_accessed=2 * slices * length * 4 * channels,
            transcendentals=0,
        ),
    )(*operands)


def after_previous(received, shard_pos, fill):
    earlier = jnp.concatenate([jnp.full_like(received[:1], fill), received[:-1]], axis=0)
    return jnp.where(shard_pos == 0, earlier, received)


def inverse_rms(values):
    width = values.shape[-1] * lax.axis_size("tensor")
    squares = lax.psum(jnp.sum(values * values, axis=-1, keepdims=True), "tensor")
    return lax.rsqrt(squares / width + epsilon)


def finish(stream, y_out, w_down, section):
    count = lax.axis_size("tensor")
    slices, rows, _ = y_out.shape
    partial = jnp.einsum("snc,cd->snd", y_out, w_down, preferred_element_type=jnp.float32)
    partial = partial.astype(jnp.bfloat16).reshape(slices, rows, count, -1)
    mixed = scatter_sum(partial, section)
    return (stream.astype(jnp.float32) + mixed).astype(jnp.bfloat16)


def one_hot(ids, vocab):
    return (ids[..., None] == jnp.arange(vocab, dtype=jnp.int32)).astype(jnp.bfloat16)


def local(token_ids, embed_table, in_proj, feat_taps, se_taps, mr_taps, out_proj, norm_gain):
    section = lax.axis_index("pipe")
    shard_pos = lax.axis_index("seq")
    shards = lax.axis_size("seq")
    vocab, width = embed_table.shape
    slices, rows = token_ids.shape
    weights = jnp.transpose(in_proj[0], (1, 0, 2))
    gain = norm_gain.astype(jnp.float32)
    ring = [(i, (i + 1) % shards) for i in range(shards)]

    share = vocab // shards
    own_rows = lax.dynamic_slice_in_dim(embed_table, shard_pos * share, share, 0).astype(jnp.float32)
    scaled = gather_features((own_rows * gain).astype(jnp.bfloat16), 0)
    own_table = project(scaled, weights, inverse_rms(own_rows))
    tables = [own_table]
    for step in range(1, shards):
        tables.append(send_on(own_table, 0, "seq", [(i, i ^ step) for i in range(shards)]))
    table = jnp.concatenate(tables, axis=0)
    prev_ids = after_previous(send_on(token_ids[:, rows - HEAD :], 0, "seq", ring), shard_pos, -1)
    ids = jnp.concatenate([prev_ids, token_ids], axis=1)
    moved = jnp.where(ids < 0, -1, ((ids // share) ^ shard_pos) * share + ids % share)
    extended = jnp.einsum(
        "snv,vc->snc", one_hot(moved, vocab), table, preferred_element_type=jnp.float32
    ).astype(jnp.bfloat16)
    embedded = jnp.einsum(
        "snv,vd->snd", one_hot(token_ids, vocab), embed_table, preferred_element_type=jnp.float32
    ).astype(jnp.bfloat16)
    y_out = mix(extended, None, feat_taps[0], se_taps)
    first = finish(embedded, y_out, out_proj[0], 0)

    stream = lax.ppermute(first, "pipe", [(0, 1)])
    values = stream.reshape(slices * rows, width).astype(jnp.float32)
    scaled = gather_features((values * gain).astype(jnp.bfloat16), 1)
    projected = project(scaled, weights, inverse_rms(values)).reshape(slices, rows, -1)
    channels = projected.shape[2] // 3
    tail = projected[:, rows - HEAD :, :]
    late = projected[:, rows - KL - KF + 1 :, channels:].astype(jnp.float32)
    kv_taps = feat_taps[0, :, 1:, :].reshape(KF, 2 * channels)
    kv_feat = sum(kv_taps[tap] * late[:, KF - 1 - tap : KF - 1 - tap + KL] for tap in range(KF))
    gated_tail = (kv_feat[:, :, :channels] * kv_feat[:, :, channels:]).astype(jnp.bfloat16)
    history = after_previous(send_on(gated_tail, 1, "seq", ring), shard_pos, 0)
    head = after_previous(send_on(tail, 1, "seq", ring), shard_pos, 0)
    extended = jnp.concatenate([head, projected], axis=1)
    y_out = mix(extended, history, feat_taps[0], mr_taps)
    second = finish(stream, y_out, out_proj[0], 1)
    return jnp.where(section == 0, first, second)[None]


def solution(mesh):
    return jax.shard_map(
        local,
        mesh=mesh,
        in_specs=(
            P(None, "seq"),
            P(None, "tensor"),
            P("pipe", None, None, "tensor"),
            P("pipe", None, None, "tensor"),
            P(None, "tensor"),
            P(None, "tensor"),
            P("pipe", "tensor", None),
            P("pipe", "tensor"),
        ),
        out_specs=P("pipe", None, "seq", "tensor"),
        check_vma=False,
    )
```

```python
import functools

import jax
import jax.numpy as jnp
from jax import lax
from jax.experimental import pallas as pl
from jax.experimental.pallas import tpu as pltpu
from jax.sharding import PartitionSpec as P

KL = 128
KS = 7
KF = 3
HEAD = 16
TAPS_AT_ONCE = 4
VMEM_LIMIT = 50 * 1024 * 1024


epsilon = 1e-06


def pairs_on(section, axis, links):
    count = lax.axis_size(axis)
    base = section * count
    return [(base + source, base + target) for source, target in links]


def send_on(value, section, axis, links):
    return lax.ppermute(value, ("pipe", axis), pairs_on(section, axis, links))


def arrivals(count):
    return [
        [sign * step for step in range(1, count) for sign in (1, -1) if 0 <= at - sign * step < count]
        for at in range(count)
    ]


def pick(moved, slot):
    count = lax.axis_size("tensor")
    place = lax.axis_index("tensor")
    order = arrivals(count)
    wanted = [order[at][slot] for at in range(count)]
    value, owner = moved[wanted[0]], jnp.int32(0) - wanted[0]
    for at in range(1, count):
        owner = jnp.where(place == at, at - wanted[at], owner)
    for hop in sorted(set(wanted) - {wanted[0]}):
        here = functools.reduce(jnp.logical_or, [place == at for at in range(count) if wanted[at] == hop])
        value = jnp.where(here, moved[hop], value)
    return value, owner


def scatter_sum(partial, section):
    count = lax.axis_size("tensor")
    place = lax.axis_index("tensor")
    if count > 4:
        own = lax.psum_scatter(partial, "tensor", scatter_dimension=0, tiled=False)
        return own.astype(jnp.float32)

    def block(index):
        index = jnp.clip(index, 0, count - 1)
        return lax.dynamic_index_in_dim(partial, index, 0, keepdims=False).astype(jnp.float32)

    up = down = None
    for step in range(1, count):
        up_block = block(count - step + place)
        down_block = block(step - count + place)
        if step > 1:
            up_block = up_block + up.astype(jnp.float32)
            down_block = down_block + down.astype(jnp.float32)
        up = send_on(up_block.astype(jnp.bfloat16), section, "tensor", [(i, i + 1) for i in range(step)])
        down = send_on(
            down_block.astype(jnp.bfloat16), section, "tensor", [(i, i - 1) for i in range(count - step, count)]
        )
    total = block(place)
    if up is not None:
        total = total + up.astype(jnp.float32) + down.astype(jnp.float32)
    return total


def project_kernel(has_base, is_last, owner_ref, x_ref, low_ref, high_ref, *refs):
    refs = list(refs)
    base_ref = refs.pop(0) if has_base else None
    inv_ref = refs.pop(0) if is_last else None
    out_ref, total = refs
    step = pl.program_id(1)
    half = low_ref.shape[1]
    rows = total.shape[0]
    product = jnp.dot(x_ref[:rows, :half], low_ref[0], preferred_element_type=jnp.float32)
    product += jnp.dot(x_ref[:rows, half:], high_ref[0], preferred_element_type=jnp.float32)

    @pl.when(step == 0)
    def _():
        total[...] = product + base_ref[...] if has_base else product

    @pl.when(step > 0)
    def _():
        total[...] += product

    @pl.when(step == pl.num_programs(1) - 1)
    def _():
        result = total[...]
        if is_last:
            result = result * inv_ref[...]
        out_ref[...] = result.astype(out_ref.dtype)


def project(chunk, owner, rows, weights, base, inv_rms):
    length, width = chunk.shape
    groups, _, channels = weights.shape
    half = min(width, 1024) // 2
    steps = width // (2 * half)
    in_specs = [
        pl.BlockSpec((length, 2 * half), lambda g, k, o: (0, k)),
        pl.BlockSpec((1, half, channels), lambda g, k, o: (g, 2 * (o[0] * steps + k), 0)),
        pl.BlockSpec((1, half, channels), lambda g, k, o: (g, 2 * (o[0] * steps + k) + 1, 0)),
    ]
    operands = [chunk, weights, weights]
    block = pl.BlockSpec((rows, channels), lambda g, k, o: (0, g))
    if base is not None:
        in_specs.append(block)
        operands.append(base)
    if inv_rms is not None:
        in_specs.append(pl.BlockSpec((rows, 1), lambda g, k, o: (0, 0)))
        operands.append(inv_rms)
    out_type = jnp.float32 if inv_rms is None else jnp.bfloat16
    return pl.pallas_call(
        functools.partial(project_kernel, base is not None, inv_rms is not None),
        grid_spec=pltpu.PrefetchScalarGridSpec(
            num_scalar_prefetch=1,
            grid=(groups, steps),
            in_specs=in_specs,
            out_specs=block,
            scratch_shapes=[pltpu.VMEM((rows, channels), jnp.float32)],
        ),
        out_shape=jax.ShapeDtypeStruct((rows, groups * channels), out_type),
        compiler_params=pltpu.CompilerParams(vmem_limit_bytes=VMEM_LIMIT),
        cost_estimate=pl.CostEstimate(
            flops=2 * rows * width * groups * channels,
            bytes_accessed=2 * (groups * width * channels + rows * width),
            transcendentals=0,
        ),
    )(owner.reshape(1).astype(jnp.int32), *operands)


def normed_projection(values, gain, weights, section):
    rows, width = values.shape
    count = lax.axis_size("tensor")
    scaled = (values * gain).astype(jnp.bfloat16)
    squares = jnp.sum(values * values, axis=1)
    ride = 1 < count <= 4 and rows <= width
    if ride:
        parts, rest = [], squares
        for _ in range(3):
            part = lax.reduce_precision(rest, 8, 7)
            parts.append(part.astype(jnp.bfloat16))
            rest = rest - part
        packed = jnp.pad(jnp.stack(parts, axis=0), ((0, 13), (0, width - rows)))
        scaled = jnp.concatenate([scaled, packed], axis=0)
    if not ride:
        inv_rms = lax.rsqrt(lax.psum(squares, "tensor") / (width * count) + epsilon)[:, None]
        gathered = lax.all_gather(scaled, "tensor", axis=1, tiled=True)
        return project(gathered, jnp.int32(0), rows, weights, None, inv_rms)

    def squares_of(chunk):
        return jnp.sum(chunk[rows : rows + 3, :rows].astype(jnp.float32), axis=0)

    moved = {0: scaled}
    chunk, owner = scaled, lax.axis_index("tensor")
    total, squares = None, squares_of(scaled)
    for step in range(1, count):
        up, down = moved[step - 1], moved[1 - step]
        moved[step] = send_on(up, section, "tensor", [(i, i + 1) for i in range(step - 1, count - 1)])
        moved[-step] = send_on(down, section, "tensor", [(i, i - 1) for i in range(1, count - step + 1)])
        total = project(chunk, owner, rows, weights, total, None)
        moved[step], moved[-step], total = lax.optimization_barrier((moved[step], moved[-step], total))
        chunk, owner = pick(moved, step - 1)
        squares = squares + squares_of(chunk)
    inv_rms = lax.rsqrt(squares / (width * count) + epsilon)[:, None]
    return project(chunk, owner, rows, weights, total, inv_rms)


def out_kernel(y_ref, w_ref, out_ref):
    product = jnp.dot(y_ref[...], w_ref[...], preferred_element_type=jnp.float32)
    out_ref[0] = product.astype(out_ref.dtype)


def out_product(y_rows, w_down):
    rows, channels = y_rows.shape
    count = lax.axis_size("tensor")
    width = w_down.shape[1] // count
    tile = min(width, 1024)
    per_block = width // tile
    return pl.pallas_call(
        out_kernel,
        grid=(count, per_block),
        in_specs=[
            pl.BlockSpec((rows, channels), lambda b, c: (0, 0)),
            pl.BlockSpec((channels, tile), lambda b, c: (0, b * per_block + c)),
        ],
        out_specs=pl.BlockSpec((1, rows, tile), lambda b, c: (b, 0, c)),
        out_shape=jax.ShapeDtypeStruct((count, rows, width), jnp.bfloat16),
        compiler_params=pltpu.CompilerParams(vmem_limit_bytes=VMEM_LIMIT),
        cost_estimate=pl.CostEstimate(
            flops=2 * rows * channels * width * count,
            bytes_accessed=2 * (channels + rows) * width * count,
            transcendentals=0,
        ),
    )(y_rows, w_down)


def mix_kernel(taps_count, has_history, *refs):
    if has_history:
        q_ref, k_ref, v_ref, history_ref, feat_ref, taps_ref, out_ref, wide, gated, shifted = refs
    else:
        q_ref, k_ref, v_ref, feat_ref, taps_ref, out_ref, wide, gated, shifted = refs
    rows = out_ref.shape[1]
    span = KL + rows

    def featured(ref, which, back):
        wide[...] = ref[0].astype(jnp.float32)
        value = jnp.zeros((back + rows, wide.shape[1]), jnp.float32)
        for tap in range(KF):
            value = value + feat_ref[tap, which : which + 1, :] * wide[
                HEAD - back - tap : HEAD - tap + rows, :
            ]
        return value

    back = 0 if has_history else 8
    gated[KL - back :, :] = featured(k_ref, 1, back) * featured(v_ref, 2, back)
    if has_history:
        gated[:KL, :] = history_ref[0].astype(jnp.float32)
    phases = min(8, taps_count)
    for phase in range(phases):
        start = 8 if has_history else KL
        shifted[phase, start:, :] = gated[start - phase : span - phase, :]

    lanes = out_ref.shape[2]
    if taps_count <= 8:
        total = jnp.zeros((rows, lanes), jnp.float32)
        for phase in range(phases):
            total = total + taps_ref[phase : phase + 1, :] * shifted[phase, KL:, :]
    else:

        def body(step, total):
            base = pl.multiple_of(step * (8 * TAPS_AT_ONCE), 8 * TAPS_AT_ONCE)
            taps = taps_ref[pl.ds(base, 8 * TAPS_AT_ONCE), :]
            start = pl.multiple_of(KL - 8 * (TAPS_AT_ONCE - 1) - base, 8)
            for phase in range(8):
                window = shifted[phase, pl.ds(start, rows + 8 * (TAPS_AT_ONCE - 1)), :]
                for late in range(TAPS_AT_ONCE):
                    offset = 8 * (TAPS_AT_ONCE - 1 - late)
                    tap = 8 * late + phase
                    total = total + taps[tap : tap + 1, :] * window[offset : offset + rows, :]
            return total

        total = lax.fori_loop(
            0, taps_count // (8 * TAPS_AT_ONCE), body, jnp.zeros((rows, lanes), jnp.float32)
        )
    out_ref[0] = (featured(q_ref, 0, 0) * total).astype(out_ref.dtype)


def mix(extended, history, feat_taps, taps):
    slices, length, wide_channels = extended.shape
    channels = wide_channels // 3
    rows = length - HEAD
    lanes = 128
    blocks = channels // lanes
    in_specs = [
        pl.BlockSpec((1, length, lanes), functools.partial(lambda g, s, c: (s, 0, g * blocks + c), g))
        for g in range(3)
    ]
    operands = [extended, extended, extended]
    if history is not None:
        in_specs.append(pl.BlockSpec((1, KL, lanes), lambda s, c: (s, 0, c)))
        operands.append(history)
    in_specs.append(pl.BlockSpec((KF, 3, lanes), lambda s, c: (0, 0, c)))
    in_specs.append(pl.BlockSpec((taps.shape[0], lanes), lambda s, c: (0, c)))
    operands += [feat_taps, taps]
    return pl.pallas_call(
        functools.partial(mix_kernel, taps.shape[0], history is not None),
        grid=(slices, blocks),
        in_specs=in_specs,
        out_specs=pl.BlockSpec((1, rows, lanes), lambda s, c: (s, 0, c)),
        out_shape=jax.ShapeDtypeStruct((slices, rows, channels), jnp.bfloat16),
        scratch_shapes=[
            pltpu.VMEM((length, lanes), jnp.float32),
            pltpu.VMEM((KL + rows, lanes), jnp.float32),
            pltpu.VMEM((8, KL + rows, lanes), jnp.float32),
        ],
        compiler_params=pltpu.CompilerParams(vmem_limit_bytes=VMEM_LIMIT),
        cost_estimate=pl.CostEstimate(
            flops=2 * taps.shape[0] * slices * rows * channels,
            bytes_accessed=2 * slices * length * 4 * channels,
            transcendentals=0,
        ),
    )(*operands)


def after_previous(received, shard_pos, fill):
    earlier = jnp.concatenate([jnp.full_like(received[:1], fill), received[:-1]], axis=0)
    return jnp.where(shard_pos == 0, earlier, received)


def finish(stream, y_out, w_down, section):
    slices, rows, channels = y_out.shape
    mixed = scatter_sum(out_product(y_out.reshape(slices * rows, channels), w_down), section)
    return (stream.astype(jnp.float32) + mixed.reshape(stream.shape)).astype(jnp.bfloat16)


def one_hot(ids, vocab):
    return (ids[..., None] == jnp.arange(vocab, dtype=jnp.int32)).astype(jnp.bfloat16)


def local(token_ids, embed_table, in_proj, feat_taps, se_taps, mr_taps, out_proj, norm_gain):
    section = lax.axis_index("pipe")
    shard_pos = lax.axis_index("seq")
    shards = lax.axis_size("seq")
    vocab, width = embed_table.shape
    slices, rows = token_ids.shape
    weights = jnp.transpose(in_proj[0], (1, 0, 2))
    gain = norm_gain.astype(jnp.float32)
    ring = [(i, (i + 1) % shards) for i in range(shards)]

    share = vocab // shards
    own_rows = lax.dynamic_slice_in_dim(embed_table, shard_pos * share, share, 0).astype(jnp.float32)
    own_table = normed_projection(own_rows, gain, weights, 0)
    tables = [own_table]
    for step in range(1, shards):
        tables.append(send_on(own_table, 0, "seq", [(i, i ^ step) for i in range(shards)]))
    table = jnp.concatenate(tables, axis=0)
    prev_ids = after_previous(send_on(token_ids[:, rows - HEAD :], 0, "seq", ring), shard_pos, -1)
    ids = jnp.concatenate([prev_ids, token_ids], axis=1)
    moved = jnp.where(ids < 0, -1, ((ids // share) ^ shard_pos) * share + ids % share)
    extended = jnp.einsum(
        "snv,vc->snc", one_hot(moved, vocab), table, preferred_element_type=jnp.float32
    ).astype(jnp.bfloat16)
    embedded = jnp.einsum(
        "snv,vd->snd", one_hot(token_ids, vocab), embed_table, preferred_element_type=jnp.float32
    ).astype(jnp.bfloat16)
    y_out = mix(extended, None, feat_taps[0], se_taps)
    first = finish(embedded, y_out, out_proj[0], 0)

    stream = lax.ppermute(first, "pipe", [(0, 1)])
    values = stream.reshape(slices * rows, width).astype(jnp.float32)
    projected = normed_projection(values, gain, weights, 1).reshape(slices, rows, -1)
    channels = projected.shape[2] // 3
    tail = projected[:, rows - HEAD :, :]
    late = projected[:, rows - KL - KF + 1 :, channels:].astype(jnp.float32)
    kv_taps = feat_taps[0, :, 1:, :].reshape(KF, 2 * channels)
    kv_feat = sum(kv_taps[tap] * late[:, KF - 1 - tap : KF - 1 - tap + KL] for tap in range(KF))
    gated_tail = (kv_feat[:, :, :channels] * kv_feat[:, :, channels:]).astype(jnp.bfloat16)
    history = after_previous(send_on(gated_tail, 1, "seq", ring), shard_pos, 0)
    head = after_previous(send_on(tail, 1, "seq", ring), shard_pos, 0)
    extended = jnp.concatenate([head, projected], axis=1)
    y_out = mix(extended, history, feat_taps[0], mr_taps)
    second = finish(stream, y_out, out_proj[0], 1)
    return jnp.where(section == 0, first, second)[None]


def solution(mesh):
    return jax.shard_map(
        local,
        mesh=mesh,
        in_specs=(
            P(None, "seq"),
            P(None, "tensor"),
            P("pipe", None, None, "tensor"),
            P("pipe", None, None, "tensor"),
            P(None, "tensor"),
            P(None, "tensor"),
            P("pipe", "tensor", None),
            P("pipe", "tensor"),
        ),
        out_specs=P("pipe", None, "seq", "tensor"),
        check_vma=False,
    )
```

```python
import functools

import jax
import jax.numpy as jnp
from jax import lax
from jax.experimental import pallas as pl
from jax.experimental.pallas import tpu as pltpu
from jax.sharding import PartitionSpec as P

KL = 128
KS = 7
KF = 3
HEAD = 16
TAPS_AT_ONCE = 4
VMEM_LIMIT = 50 * 1024 * 1024


epsilon = 1e-06


def pairs_on(section, axis, links):
    count = lax.axis_size(axis)
    base = section * count
    return [(base + source, base + target) for source, target in links]


def send_on(value, section, axis, links):
    return lax.ppermute(value, ("pipe", axis), pairs_on(section, axis, links))


def arrivals(count):
    return [
        [sign * step for step in range(1, count) for sign in (1, -1) if 0 <= at - sign * step < count]
        for at in range(count)
    ]


def pick(moved, slot):
    count = lax.axis_size("tensor")
    place = lax.axis_index("tensor")
    order = arrivals(count)
    wanted = [order[at][slot] for at in range(count)]
    value, owner = moved[wanted[0]], jnp.int32(0) - wanted[0]
    for at in range(1, count):
        owner = jnp.where(place == at, at - wanted[at], owner)
    for hop in sorted(set(wanted) - {wanted[0]}):
        here = functools.reduce(jnp.logical_or, [place == at for at in range(count) if wanted[at] == hop])
        value = jnp.where(here, moved[hop], value)
    return value, owner


def scatter_sum(partial, section):
    count = lax.axis_size("tensor")
    place = lax.axis_index("tensor")
    if count > 4:
        own = lax.psum_scatter(partial, "tensor", scatter_dimension=0, tiled=False)
        return own.astype(jnp.float32)

    def block(index):
        index = jnp.clip(index, 0, count - 1)
        return lax.dynamic_index_in_dim(partial, index, 0, keepdims=False).astype(jnp.float32)

    up = down = None
    for step in range(1, count):
        up_block = block(count - step + place)
        down_block = block(step - count + place)
        if step > 1:
            up_block = up_block + up.astype(jnp.float32)
            down_block = down_block + down.astype(jnp.float32)
        up = send_on(up_block.astype(jnp.bfloat16), section, "tensor", [(i, i + 1) for i in range(step)])
        down = send_on(
            down_block.astype(jnp.bfloat16), section, "tensor", [(i, i - 1) for i in range(count - step, count)]
        )
    total = block(place)
    if up is not None:
        total = total + up.astype(jnp.float32) + down.astype(jnp.float32)
    return total


def project_kernel(has_base, is_last, owner_ref, x_ref, low_ref, high_ref, *refs):
    refs = list(refs)
    base_ref = refs.pop(0) if has_base else None
    inv_ref = refs.pop(0) if is_last else None
    out_ref, total = refs
    step = pl.program_id(1)
    half = low_ref.shape[1]
    rows = total.shape[0]
    product = jnp.dot(x_ref[:rows, :half], low_ref[0], preferred_element_type=jnp.float32)
    product += jnp.dot(x_ref[:rows, half:], high_ref[0], preferred_element_type=jnp.float32)

    @pl.when(step == 0)
    def _():
        total[...] = product + base_ref[...] if has_base else product

    @pl.when(step > 0)
    def _():
        total[...] += product

    @pl.when(step == pl.num_programs(1) - 1)
    def _():
        result = total[...]
        if is_last:
            result = result * inv_ref[...]
        out_ref[...] = result.astype(out_ref.dtype)


def project(chunk, owner, rows, weights, base, inv_rms):
    length, width = chunk.shape
    groups, _, channels = weights.shape
    half = min(width, 1024) // 2
    steps = width // (2 * half)
    in_specs = [
        pl.BlockSpec((length, 2 * half), lambda g, k, o: (0, k)),
        pl.BlockSpec((1, half, channels), lambda g, k, o: (g, 2 * (o[0] * steps + k), 0)),
        pl.BlockSpec((1, half, channels), lambda g, k, o: (g, 2 * (o[0] * steps + k) + 1, 0)),
    ]
    operands = [chunk, weights, weights]
    block = pl.BlockSpec((rows, channels), lambda g, k, o: (0, g))
    if base is not None:
        in_specs.append(block)
        operands.append(base)
    if inv_rms is not None:
        in_specs.append(pl.BlockSpec((rows, 1), lambda g, k, o: (0, 0)))
        operands.append(inv_rms)
    out_type = jnp.float32 if inv_rms is None else jnp.bfloat16
    return pl.pallas_call(
        functools.partial(project_kernel, base is not None, inv_rms is not None),
        grid_spec=pltpu.PrefetchScalarGridSpec(
            num_scalar_prefetch=1,
            grid=(groups, steps),
            in_specs=in_specs,
            out_specs=block,
            scratch_shapes=[pltpu.VMEM((rows, channels), jnp.float32)],
        ),
        out_shape=jax.ShapeDtypeStruct((rows, groups * channels), out_type),
        compiler_params=pltpu.CompilerParams(vmem_limit_bytes=VMEM_LIMIT),
        cost_estimate=pl.CostEstimate(
            flops=2 * rows * width * groups * channels,
            bytes_accessed=2 * (groups * width * channels + rows * width),
            transcendentals=0,
        ),
    )(owner.reshape(1).astype(jnp.int32), *operands)


def normed_projection(values, gain, weights, section):
    rows, width = values.shape
    count = lax.axis_size("tensor")
    scaled = (values * gain).astype(jnp.bfloat16)
    squares = jnp.sum(values * values, axis=1)
    ride = 1 < count <= 4 and rows <= width
    if ride:
        parts, rest = [], squares
        for _ in range(3):
            part = lax.reduce_precision(rest, 8, 7)
            parts.append(part.astype(jnp.bfloat16))
            rest = rest - part
        packed = jnp.pad(jnp.stack(parts, axis=0), ((0, 13), (0, width - rows)))
        scaled = jnp.concatenate([scaled, packed], axis=0)
    if not ride:
        inv_rms = lax.rsqrt(lax.psum(squares, "tensor") / (width * count) + epsilon)[:, None]
        gathered = lax.all_gather(scaled, "tensor", axis=1, tiled=True)
        return project(gathered, jnp.int32(0), rows, weights, None, inv_rms)

    def squares_of(chunk):
        return jnp.sum(chunk[rows : rows + 3, :rows].astype(jnp.float32), axis=0)

    moved = {0: scaled}
    chunk, owner = scaled, lax.axis_index("tensor")
    total, squares = None, squares_of(scaled)
    for step in range(1, count):
        up, down = moved[step - 1], moved[1 - step]
        moved[step] = send_on(up, section, "tensor", [(i, i + 1) for i in range(step - 1, count - 1)])
        moved[-step] = send_on(down, section, "tensor", [(i, i - 1) for i in range(1, count - step + 1)])
        total = project(chunk, owner, rows, weights, total, None)
        moved[step], moved[-step], total = lax.optimization_barrier((moved[step], moved[-step], total))
        chunk, owner = pick(moved, step - 1)
        squares = squares + squares_of(chunk)
    inv_rms = lax.rsqrt(squares / (width * count) + epsilon)[:, None]
    return project(chunk, owner, rows, weights, total, inv_rms)


def out_kernel(y_ref, low_ref, high_ref, out_ref):
    half = low_ref.shape[0]
    product = jnp.dot(y_ref[:, :half], low_ref[...], preferred_element_type=jnp.float32)
    product += jnp.dot(y_ref[:, half:], high_ref[...], preferred_element_type=jnp.float32)
    out_ref[0] = product.astype(out_ref.dtype)


def out_product(y_rows, w_down):
    rows, channels = y_rows.shape
    count = lax.axis_size("tensor")
    width = w_down.shape[1] // count
    tile = min(width, 1024)
    per_block = width // tile
    return pl.pallas_call(
        out_kernel,
        grid=(count, per_block),
        in_specs=[
            pl.BlockSpec((rows, channels), lambda b, c: (0, 0)),
            pl.BlockSpec((channels // 2, tile), lambda b, c: (0, b * per_block + c)),
            pl.BlockSpec((channels // 2, tile), lambda b, c: (1, b * per_block + c)),
        ],
        out_specs=pl.BlockSpec((1, rows, tile), lambda b, c: (b, 0, c)),
        out_shape=jax.ShapeDtypeStruct((count, rows, width), jnp.bfloat16),
        compiler_params=pltpu.CompilerParams(vmem_limit_bytes=VMEM_LIMIT),
        cost_estimate=pl.CostEstimate(
            flops=2 * rows * channels * width * count,
            bytes_accessed=2 * (channels + rows) * width * count,
            transcendentals=0,
        ),
    )(y_rows, w_down, w_down)


def mix_kernel(taps_count, has_history, *refs):
    if has_history:
        q_ref, k_ref, v_ref, history_ref, feat_ref, taps_ref, out_ref, wide, gated, shifted = refs
    else:
        q_ref, k_ref, v_ref, feat_ref, taps_ref, out_ref, wide, gated, shifted = refs
    rows = out_ref.shape[1]
    span = KL + rows

    def featured(ref, which, back):
        wide[...] = ref[0].astype(jnp.float32)
        value = jnp.zeros((back + rows, wide.shape[1]), jnp.float32)
        for tap in range(KF):
            value = value + feat_ref[tap, which : which + 1, :] * wide[
                HEAD - back - tap : HEAD - tap + rows, :
            ]
        return value

    back = 0 if has_history else 8
    gated[KL - back :, :] = featured(k_ref, 1, back) * featured(v_ref, 2, back)
    if has_history:
        gated[:KL, :] = history_ref[0].astype(jnp.float32)
    phases = min(8, taps_count)
    for phase in range(phases):
        start = 8 if has_history else KL
        shifted[phase, start:, :] = gated[start - phase : span - phase, :]

    lanes = out_ref.shape[2]
    if taps_count <= 8:
        total = jnp.zeros((rows, lanes), jnp.float32)
        for phase in range(phases):
            total = total + taps_ref[phase : phase + 1, :] * shifted[phase, KL:, :]
    else:

        def body(step, total):
            base = pl.multiple_of(step * (8 * TAPS_AT_ONCE), 8 * TAPS_AT_ONCE)
            taps = taps_ref[pl.ds(base, 8 * TAPS_AT_ONCE), :]
            start = pl.multiple_of(KL - 8 * (TAPS_AT_ONCE - 1) - base, 8)
            for phase in range(8):
                window = shifted[phase, pl.ds(start, rows + 8 * (TAPS_AT_ONCE - 1)), :]
                for late in range(TAPS_AT_ONCE):
                    offset = 8 * (TAPS_AT_ONCE - 1 - late)
                    tap = 8 * late + phase
                    total = total + taps[tap : tap + 1, :] * window[offset : offset + rows, :]
            return total

        total = lax.fori_loop(
            0, taps_count // (8 * TAPS_AT_ONCE), body, jnp.zeros((rows, lanes), jnp.float32)
        )
    out_ref[0] = (featured(q_ref, 0, 0) * total).astype(out_ref.dtype)


def mix(extended, history, feat_taps, taps, part):
    _, length, wide_channels = extended.shape
    channels = wide_channels // 3
    rows = length - HEAD
    lanes = 128
    blocks = channels // lanes
    in_specs = [
        pl.BlockSpec((1, length, lanes), functools.partial(lambda g, c: (part, 0, g * blocks + c), g))
        for g in range(3)
    ]
    operands = [extended, extended, extended]
    if history is not None:
        in_specs.append(pl.BlockSpec((1, KL, lanes), lambda c: (part, 0, c)))
        operands.append(history)
    in_specs.append(pl.BlockSpec((KF, 3, lanes), lambda c: (0, 0, c)))
    in_specs.append(pl.BlockSpec((taps.shape[0], lanes), lambda c: (0, c)))
    operands += [feat_taps, taps]
    return pl.pallas_call(
        functools.partial(mix_kernel, taps.shape[0], history is not None),
        grid=(blocks,),
        in_specs=in_specs,
        out_specs=pl.BlockSpec((1, rows, lanes), lambda c: (0, 0, c)),
        out_shape=jax.ShapeDtypeStruct((1, rows, channels), jnp.bfloat16),
        scratch_shapes=[
            pltpu.VMEM((length, lanes), jnp.float32),
            pltpu.VMEM((KL + rows, lanes), jnp.float32),
            pltpu.VMEM((8, KL + rows, lanes), jnp.float32),
        ],
        compiler_params=pltpu.CompilerParams(vmem_limit_bytes=VMEM_LIMIT),
        cost_estimate=pl.CostEstimate(
            flops=2 * taps.shape[0] * rows * channels,
            bytes_accessed=2 * length * 4 * channels,
            transcendentals=0,
        ),
    )(*operands)


def after_previous(received, shard_pos, fill):
    earlier = jnp.concatenate([jnp.full_like(received[:1], fill), received[:-1]], axis=0)
    return jnp.where(shard_pos == 0, earlier, received)


def finish(stream, y_out, w_down, section):
    mixed = scatter_sum(out_product(y_out[0], w_down), section)
    return (stream.astype(jnp.float32) + mixed).astype(jnp.bfloat16)


def one_hot(ids, vocab):
    return (ids[..., None] == jnp.arange(vocab, dtype=jnp.int32)).astype(jnp.bfloat16)


def local(token_ids, embed_table, in_proj, feat_taps, se_taps, mr_taps, out_proj, norm_gain):
    section = lax.axis_index("pipe")
    shard_pos = lax.axis_index("seq")
    shards = lax.axis_size("seq")
    vocab, width = embed_table.shape
    slices, rows = token_ids.shape
    weights = jnp.transpose(in_proj[0], (1, 0, 2))
    gain = norm_gain.astype(jnp.float32)
    ring = [(i, (i + 1) % shards) for i in range(shards)]

    share = vocab // shards
    own_rows = lax.dynamic_slice_in_dim(embed_table, shard_pos * share, share, 0).astype(jnp.float32)
    own_table = normed_projection(own_rows, gain, weights, 0)
    tables = [own_table]
    for step in range(1, shards):
        tables.append(send_on(own_table, 0, "seq", [(i, i ^ step) for i in range(shards)]))
    table = jnp.concatenate(tables, axis=0)
    prev_ids = after_previous(send_on(token_ids[:, rows - HEAD :], 0, "seq", ring), shard_pos, -1)
    ids = jnp.concatenate([prev_ids, token_ids], axis=1)
    moved = jnp.where(ids < 0, -1, ((ids // share) ^ shard_pos) * share + ids % share)
    extended = jnp.einsum(
        "snv,vc->snc", one_hot(moved, vocab), table, preferred_element_type=jnp.float32
    ).astype(jnp.bfloat16)
    embedded = jnp.einsum(
        "snv,vd->snd", one_hot(token_ids, vocab), embed_table, preferred_element_type=jnp.float32
    ).astype(jnp.bfloat16)
    firsts = []
    for part in range(slices):
        y_out = mix(extended, None, feat_taps[0], se_taps, part)
        firsts.append(finish(embedded[part], y_out, out_proj[0], 0))

    streams = [lax.ppermute(first, "pipe", [(0, 1)]) for first in firsts]
    values = jnp.concatenate(streams, axis=0).astype(jnp.float32)
    projected = normed_projection(values, gain, weights, 1).reshape(slices, rows, -1)
    channels = projected.shape[2] // 3
    tail = projected[:, rows - HEAD :, :]
    late = projected[:, rows - KL - KF + 1 :, channels:].astype(jnp.float32)
    kv_taps = feat_taps[0, :, 1:, :].reshape(KF, 2 * channels)
    kv_feat = sum(kv_taps[tap] * late[:, KF - 1 - tap : KF - 1 - tap + KL] for tap in range(KF))
    gated_tail = (kv_feat[:, :, :channels] * kv_feat[:, :, channels:]).astype(jnp.bfloat16)
    history = after_previous(send_on(gated_tail, 1, "seq", ring), shard_pos, 0)
    head = after_previous(send_on(tail, 1, "seq", ring), shard_pos, 0)
    extended = jnp.concatenate([head, projected], axis=1)
    outputs = []
    for part in range(slices):
        y_out = mix(extended, history, feat_taps[0], mr_taps, part)
        second = finish(streams[part], y_out, out_proj[0], 1)
        outputs.append(jnp.where(section == 0, firsts[part], second))
    return jnp.stack(outputs, axis=0)[None]


def solution(mesh):
    return jax.shard_map(
        local,
        mesh=mesh,
        in_specs=(
            P(None, "seq"),
            P(None, "tensor"),
            P("pipe", None, None, "tensor"),
            P("pipe", None, None, "tensor"),
            P(None, "tensor"),
            P(None, "tensor"),
            P("pipe", "tensor", None),
            P("pipe", "tensor"),
        ),
        out_specs=P("pipe", None, "seq", "tensor"),
        check_vma=False,
    )
```
